32 devices in a mesh: sec: 4 (over y, x), dom: 8 (over z, core).
Axes of the slice: x: 2, y: 2, z: 4, core: 2. Of those that a mesh axis runs over, the one named last changes fastest.
Arguments:
- fields: float32 [4, 64, 8192], P(None, None, ('sec', 'dom')), may hold values from -6 to 6
- source_map: int32 [8192], P(('sec', 'dom')), may hold values from 0 to 255
- new_owner: int32 [2048], P(('sec', 'dom')), may hold values from 0 to 7, as said below
- send_list: int32 [3072], P(('sec', 'dom')), may hold values from -1 to 1535, as said below
- face_slot: int32 [6, 8192], P(None, ('sec', 'dom')), may hold values from -1 to 1631, as said below
Outputs:
- advanced: float32 [4, 64, 8192], P(None, None, ('sec', 'dom'))
The draws below stay inside these ranges and needn't reach their ends.
Inputs may be any that keep to these rules, and one draw needn't show every extreme that they name: source_map names a cell block of the flow device with the same dom index. new_owner names a device of the same section within 2 dom indices; two devices trade as many blocks each way, at most 4; in every section some device trades exactly 4 with each of its 4 nearby devices. send_list holds, for each device, 4 lists of 24 entries for the offsets -2 to -1 and 1 to 2; an entry f * 256 + e names face f of local element e; a list for a device inside the section is full, one for a device outside it is -1. face_slot names for every element face the touching face: the opposite end along the same direction, nodes in the same order, on the same device or in the lists of a device within 2; -1 marks the outer boundary.
All inputs are finite; a program needn't handle non-finite values.
Results may differ from the reference program's by a relative error of at most 0.0003.
Values sent between devices are 32-bit elements; how exact they have to be, the bound alone decides.
A program may use at most 64 MiB of HBM per device.

```python
import jax
import jax.numpy as jnp
import numpy as np
from jax import lax

ELEMENTS = 256
BLOCK_SIZE = 4
MOVE_CAP = 4
SPREAD = 2
CHAIN_LEN = 8
CHAIN_SENDS = 4
BLOCKS = 64
FACE_CAP = 24
ALL_ELEMENTS = 8192
N_SEC = 4
N_DOM = 8


def owner_section(key):
    pair_key, star_key, perm_key = jax.random.split(key, 3)
    trades = jax.random.randint(pair_key, (N_DOM, SPREAD), 0, MOVE_CAP + 1)
    device = jnp.arange(N_DOM)
    reach = jnp.arange(1, SPREAD + 1)
    inside = device[:, None] + reach[None, :] < N_DOM
    star = jax.random.randint(star_key, (), SPREAD, N_DOM - SPREAD)
    forced = (device[:, None] == star) | (device[:, None] + reach[None, :] == star)
    trades = jnp.where(forced, MOVE_CAP, trades)
    trades = jnp.where(inside, trades, 0)
    downward = jnp.stack([jnp.where(device - offset_value >= 0, trades[jnp.clip(device - offset_value, 0), offset_value - 1], 0) for offset_value in range(SPREAD, 0, -1)], axis=1)
    counts = jnp.concatenate([downward, trades], axis=1)
    offsets = jnp.concatenate([jnp.arange(-SPREAD, 0), jnp.arange(1, SPREAD + 1)])
    running = jnp.cumsum(counts, axis=1)
    position = jnp.arange(BLOCKS)
    slot_number = jnp.sum(position[None, :, None] >= running[:, None, :], axis=2)
    target = jnp.where(slot_number < 2 * SPREAD, device[:, None] + offsets[jnp.clip(slot_number, 0, 2 * SPREAD - 1)], device[:, None])
    shuffles = jax.vmap(lambda subkey: jax.random.permutation(subkey, BLOCKS))(jax.random.split(perm_key, N_DOM))
    return jnp.take_along_axis(target, shuffles, axis=1).reshape(-1).astype(jnp.int32)


def draw_new_owner(key, part):
    sections = jax.vmap(lambda number: owner_section(jax.random.fold_in(key, number)))(jnp.arange(N_SEC))
    return sections.reshape(-1).astype(jnp.int32)


def slot_of(offset_value):
    return jnp.where(offset_value < 0, offset_value + SPREAD, offset_value + SPREAD - 1)


def face_section(key):
    offsets = jnp.concatenate([jnp.arange(-SPREAD, 0), jnp.arange(1, SPREAD + 1)])
    chains = ELEMENTS // CHAIN_LEN
    device = jnp.arange(N_DOM)
    rows = device[:, None]
    dump = 2 * SPREAD * FACE_CAP
    slots = jnp.full((N_DOM, 6, ELEMENTS), -1, jnp.int32)
    sends = jnp.full((N_DOM, dump + 1), -1, jnp.int32)
    for direction in range(3):
        axis_key = jax.random.fold_in(key, direction)
        shuffles = jax.vmap(lambda subkey: jax.random.permutation(subkey, ELEMENTS))(jax.random.split(jax.random.fold_in(axis_key, 1), N_DOM))
        base = jnp.concatenate([jnp.zeros(chains - 2 * SPREAD * CHAIN_SENDS, jnp.int32), jnp.repeat(offsets, CHAIN_SENDS).astype(jnp.int32)])
        chain_off = jax.random.permutation(jax.random.fold_in(axis_key, 2), base)
        links = shuffles.reshape(N_DOM, chains, CHAIN_LEN)
        lower = 2 * direction
        upper = 2 * direction + 1
        left = links[:, :, :-1].reshape(N_DOM, -1)
        right = links[:, :, 1:].reshape(N_DOM, -1)
        slots = slots.at[rows, upper, left].set(lower * ELEMENTS + right)
        slots = slots.at[rows, lower, right].set(upper * ELEMENTS + left)
        ends = links[:, :, -1]
        starts = links[:, :, 0]
        match = (chain_off[:, None] == offsets[None, :]).astype(jnp.int32)
        ranking = jnp.sum((jnp.cumsum(match, axis=0) - 1) * match, axis=1)
        own_slot = slot_of(chain_off)
        back_slot = slot_of(-chain_off)
        target = device[:, None] + chain_off[None, :]
        source = device[:, None] - chain_off[None, :]
        upward_ok = (target >= 0) & (target < N_DOM)
        downward_ok = (source >= 0) & (source < N_DOM)
        local = (chain_off == 0)[None, :]
        remote_upper = 6 * ELEMENTS + own_slot * FACE_CAP + direction * 2 * CHAIN_SENDS + CHAIN_SENDS + ranking
        remote_lower = 6 * ELEMENTS + back_slot * FACE_CAP + direction * 2 * CHAIN_SENDS + ranking
        upper_value = jnp.where(local, lower * ELEMENTS + starts, jnp.where(upward_ok, remote_upper[None, :], -1))
        lower_value = jnp.where(local, upper * ELEMENTS + ends, jnp.where(downward_ok, remote_lower[None, :], -1))
        slots = slots.at[rows, upper, ends].set(upper_value.astype(jnp.int32))
        slots = slots.at[rows, lower, starts].set(lower_value.astype(jnp.int32))
        end_place = jnp.where(local | ~upward_ok, dump, (own_slot * FACE_CAP + direction * 2 * CHAIN_SENDS + ranking)[None, :])
        sends = sends.at[rows, end_place].set(upper * ELEMENTS + ends)
        start_place = jnp.where(local | ~downward_ok, dump, (back_slot * FACE_CAP + direction * 2 * CHAIN_SENDS + CHAIN_SENDS + ranking)[None, :])
        sends = sends.at[rows, start_place].set(lower * ELEMENTS + starts)
    return (sends[:, :dump], slots)


def face_lists(key):
    return jax.vmap(lambda number: face_section(jax.random.fold_in(key, number)))(jnp.arange(N_SEC))


def draw_send_list(key, part):
    sends, slots = face_lists(key)
    return sends.reshape(-1).astype(jnp.int32)


def draw_face_slot(key, part):
    sends, slots = face_lists(key)
    return jnp.transpose(slots, (2, 0, 1, 3)).reshape(6, -1).astype(jnp.int32)


def touch_ends(values, stream_key, low, largest):
    dims = values.shape
    index_at = [jax.random.randint(jax.random.fold_in(stream_key, axis), (), 0, dims[axis]) for axis in range(len(dims))]
    values = values.at[tuple(index_at)].set(low)
    longest = dims.index(max(dims))
    index_at[longest] = (index_at[longest] + 1) % dims[longest]
    return values.at[tuple(index_at)].set(largest)


def levels(key, dims, shards, least, high):
    def one(dim, blocks):
        steps = jax.random.uniform(jax.random.fold_in(jax.random.fold_in(key, 6), dim), (blocks,), jnp.float32, least / len(shards), high / len(shards))
        return jnp.repeat(jnp.exp(steps), dims[dim] // blocks).reshape((-1,) + (1,) * (len(dims) - dim - 1))

    loudness = one(*shards[0])
    for cut in shards[1:]:
        loudness = loudness * one(*cut)
    return loudness


def normal_values(stream_key, dims, deviation, limit, cuts=(), held_as=jnp.bfloat16):
    gain = levels(stream_key, dims, cuts, -0.22, 0.18) if cuts else 1.0
    drawn = jax.random.normal(stream_key, dims, jnp.float32) * deviation * gain
    return jnp.minimum(jnp.maximum(drawn, -limit), limit).astype(held_as)


def setup_inputs(seed: int = 0) -> dict:
    key_of = jax.random.split(jax.random.key(seed), 6)
    return {
        "fields": normal_values(key_of[0], (4, 64, ALL_ELEMENTS), 1.0, 6.0, ((2, 32),), jnp.float32),
        "source_map": touch_ends(jax.random.randint(key_of[1], (ALL_ELEMENTS,), 0, ELEMENTS), jax.random.fold_in(key_of[1], 1), 0, ELEMENTS - 1).astype(jnp.int32),
        "new_owner": draw_new_owner(jax.random.fold_in(key_of[5], 71), 0),
        "send_list": draw_send_list(jax.random.fold_in(key_of[5], 71), 0),
        "face_slot": draw_face_slot(jax.random.fold_in(key_of[5], 71), 0),
    }


CELL_DIFFERENCE = [[-1.0, 1.0, 0.0, 0.0], [-0.5, 0.0, 0.5, 0.0], [0.0, -0.5, 0.0, 0.5], [0.0, 0.0, -1.0, 1.0]]
SEGMENT_CARRY = [0.0, -567301805773.0 / 1357537059087.0, -2404267990393.0 / 2016746695238.0, -3550918686646.0 / 2091501179385.0, -1275806237668.0 / 842570457699.0]
SEGMENT_WEIGHTS = [1432997174477.0 / 9575080441755.0, 5161836677717.0 / 13612068292357.0, 1720146321549.0 / 2090206949498.0, 3134564353537.0 / 4481467310338.0, 2277821191437.0 / 14882151754819.0]
TIME_STEP = 0.12
END_LIFT = 6.0

def node_derivative():
    points = np.array([-1.0, -1.0 / np.sqrt(5.0), 1.0 / np.sqrt(5.0), 1.0])
    products = np.array([np.prod([points[row] - points[col] for col in range(4) if col != row]) for row in range(4)])
    matrix = np.zeros((4, 4))
    for row in range(4):
        for col in range(4):
            if row != col:
                matrix[row, col] = products[row] / (products[col] * (points[row] - points[col]))
        matrix[row, row] = -np.sum(matrix[row])
    return matrix

def derivative_along(matrix, field, direction):
    forms = ['mi,ijke->mjke', 'mj,ijke->imke', 'mk,ijke->ijme']
    return jnp.einsum(forms[direction], matrix, field, precision=lax.Precision.HIGHEST)

def lamb_vector(cells):
    cube = cells.reshape(4, 4, 4, 4, -1)
    matrix = jnp.asarray(CELL_DIFFERENCE, cells.dtype)

    def slope(component, direction):
        return derivative_along(matrix, cube[component], direction)
    spin_x = slope(2, 1) - slope(1, 2)
    spin_y = slope(0, 2) - slope(2, 0)
    spin_z = slope(1, 0) - slope(0, 1)
    lamb_x = spin_y * cube[2] - spin_z * cube[1]
    lamb_y = spin_z * cube[0] - spin_x * cube[2]
    lamb_z = spin_x * cube[1] - spin_y * cube[0]
    return (cube[3] * jnp.stack([lamb_x, lamb_y, lamb_z])).reshape(3, 64, -1)

def face_traces(state_now):
    cube = state_now.reshape(4, 4, 4, 4, -1)
    faces = [cube[:, 0], cube[:, 3], cube[:, :, 0], cube[:, :, 3], cube[:, :, :, 0], cube[:, :, :, 3]]
    return jnp.stack([piece.reshape(4, 16, -1) for piece in faces], axis=2).reshape(4, 16, -1)

def exterior(traces, received, slots_here):
    lookup = jnp.concatenate([traces, received], axis=2)
    flat_slots = slots_here.reshape(-1)
    outside = jnp.take(lookup, jnp.clip(flat_slots, 0), axis=2) * (flat_slots >= 0)
    return outside.reshape(4, 16, 6, -1)

def tendency(state_now, traces, outside, forcing):
    elements = state_now.shape[2]
    cube = state_now.reshape(4, 4, 4, 4, elements)
    matrix = jnp.asarray(node_derivative(), state_now.dtype)
    divergence = derivative_along(matrix, cube[1], 0) + derivative_along(matrix, cube[2], 1) + derivative_along(matrix, cube[3], 2)
    force_cube = forcing.reshape(3, 4, 4, 4, elements)
    pieces = [-divergence] + [force_cube[direction] - derivative_along(matrix, cube[0], direction) for direction in range(3)]
    result = jnp.stack(pieces)
    inside = traces.reshape(4, 16, 6, elements)
    for direction in range(3):
        for face_side in range(2):
            face_index = 2 * direction + face_side
            normal_sign = 2.0 * face_side - 1.0
            jump_value = outside[:, :, face_index] - inside[:, :, face_index]
            correction = 0.5 * jump_value
            correction = correction.at[0].add(-0.5 * normal_sign * jump_value[1 + direction])
            correction = correction.at[1 + direction].add(-0.5 * normal_sign * jump_value[0])
            lifted = (END_LIFT * correction).reshape(4, 4, 4, elements)
            where_index = (slice(None),) * (direction + 1) + (3 * face_side,)
            result = result.at[where_index].add(lifted)
    return result.reshape(4, 64, elements)

def reference(fields, source_map, new_owner, send_list, face_slot):
    sections = N_SEC
    domains = N_DOM
    elements = ELEMENTS
    blocks = BLOCKS
    devices = sections * domains
    slot_total = 2 * SPREAD * FACE_CAP
    lamb_source = lamb_vector(fields[:, :, :domains * elements])
    section_maps = source_map.reshape(sections, domains, elements)
    flat_source = (jnp.arange(domains, dtype=jnp.int32)[None, :, None] * elements + section_maps).reshape(-1).astype(jnp.int32)
    forcing_cols = jnp.take(lamb_source, flat_source, axis=2)
    packed = jnp.concatenate([fields, forcing_cols], axis=0)
    owners = new_owner.reshape(sections, domains * blocks)
    block_ids = jnp.arange(domains * blocks, dtype=jnp.int32)
    source_dom = block_ids // blocks
    local_block = block_ids % blocks
    step_away = source_dom[None, :] - owners
    rank_group = jnp.where(step_away == 0, 0, step_away + SPREAD + 1)
    sort_key = owners * ((2 * SPREAD + 2) * blocks) + rank_group * blocks + local_block[None, :]
    new_order = jnp.argsort(sort_key, axis=1).astype(jnp.int32)
    element_src = (new_order[:, :, None] * BLOCK_SIZE + jnp.arange(BLOCK_SIZE, dtype=jnp.int32)[None, None, :]).reshape(sections, -1)
    element_src = element_src + (jnp.arange(sections, dtype=jnp.int32) * (domains * elements))[:, None]
    placed = jnp.take(packed, element_src.reshape(-1).astype(jnp.int32), axis=2)
    state_now = placed[:4]
    forcing = placed[4:]
    carry_rate = jnp.zeros_like(state_now)
    send_rows = send_list.reshape(devices, slot_total)
    offsets = [value for value in range(-SPREAD, SPREAD + 1) if value != 0]
    device_ids = jnp.arange(devices, dtype=jnp.int32)
    for segment_index in range(5):

        def gather_sent(item):
            device_id, send_row = item
            local = lax.dynamic_slice_in_dim(state_now, device_id * elements, elements, 2)
            traces = face_traces(local)
            return jnp.take(traces, jnp.clip(send_row, 0), axis=2) * (send_row >= 0)
        sent = lax.map(gather_sent, (device_ids, send_rows))
        sent = sent.reshape(sections, domains, 4, 16, 2 * SPREAD, FACE_CAP)
        incoming = []
        for slot_index, offset_value in enumerate(offsets):
            piece = sent[:, :, :, :, 2 * SPREAD - 1 - slot_index]
            if offset_value > 0:
                piece = jnp.concatenate([piece[:, offset_value:], jnp.zeros_like(piece[:, :offset_value])], axis=1)
            else:
                back = -offset_value
                piece = jnp.concatenate([jnp.zeros_like(piece[:, :back]), piece[:, :-back]], axis=1)
            incoming.append(piece)
        received = jnp.stack(incoming, axis=4).reshape(devices, 4, 16, slot_total)

        def device_rate(item):
            device_id, recv_block = item
            local = lax.dynamic_slice_in_dim(state_now, device_id * elements, elements, 2)
            local_force = lax.dynamic_slice_in_dim(forcing, device_id * elements, elements, 2)
            slots_here = lax.dynamic_slice_in_dim(face_slot, device_id * elements, elements, 1)
            traces = face_traces(local)
            outside = exterior(traces, recv_block, slots_here)
            rate_here = tendency(local, traces, outside, local_force)
            return jnp.where(device_id >= domains, rate_here, jnp.zeros_like(rate_here))
        rates = lax.map(device_rate, (device_ids, received))
        rates = jnp.transpose(rates, (1, 2, 0, 3)).reshape(4, 64, -1)
        carry_rate = SEGMENT_CARRY[segment_index] * carry_rate + TIME_STEP * rates
        state_now = state_now + SEGMENT_WEIGHTS[segment_index] * carry_rate
    return state_now
```

```python
import functools

import jax
import jax.numpy as jnp
import numpy as np
from jax import lax
from jax.experimental import pallas as pl
from jax.experimental.pallas import tpu as pltpu
from jax.sharding import PartitionSpec as P

BLOCK_SIZE = 4
MOVE_CAP = 4
SPREAD = 2
FACE_CAP = 24
MOVE = MOVE_CAP * BLOCK_SIZE
PEERS = 2 * SPREAD
LANES = 128
TRACE = 48
OFFSETS = [value for value in range(-SPREAD, SPREAD + 1) if value != 0]

CELL_DIFFERENCE = [
    [-1.0, 1.0, 0.0, 0.0],
    [-0.5, 0.0, 0.5, 0.0],
    [0.0, -0.5, 0.0, 0.5],
    [0.0, 0.0, -1.0, 1.0],
]
SEGMENT_CARRY = [
    0.0,
    -567301805773.0 / 1357537059087.0,
    -2404267990393.0 / 2016746695238.0,
    -3550918686646.0 / 2091501179385.0,
    -1275806237668.0 / 842570457699.0,
]
SEGMENT_WEIGHTS = [
    1432997174477.0 / 9575080441755.0,
    5161836677717.0 / 13612068292357.0,
    1720146321549.0 / 2090206949498.0,
    3134564353537.0 / 4481467310338.0,
    2277821191437.0 / 14882151754819.0,
]
SEGMENTS = len(SEGMENT_CARRY)
TIME_STEP = 0.12
END_LIFT = 6.0
F32 = jnp.float32
BF16 = jnp.bfloat16
MESH = pl.DeviceIdType.MESH


def node_derivative():
    points = np.array([-1.0, -1.0 / np.sqrt(5.0), 1.0 / np.sqrt(5.0), 1.0])
    products = np.array(
        [np.prod([points[row] - points[col] for col in range(4) if col != row]) for row in range(4)]
    )
    matrix = np.zeros((4, 4))
    for row in range(4):
        for col in range(4):
            if row != col:
                matrix[row, col] = products[row] / (products[col] * (points[row] - points[col]))
        matrix[row, row] = -np.sum(matrix[row])
    return matrix


def along(matrix, direction):
    parts = [np.eye(4)] * 3
    parts[direction] = matrix
    return np.kron(np.kron(parts[0], parts[1]), parts[2])


def face_nodes(direction, side):
    cube = np.arange(64).reshape(4, 4, 4)
    return np.take(cube, 3 * side, axis=direction).reshape(-1)


def constants():
    deriv = node_derivative()
    own = np.zeros((256, 256))
    lift = np.zeros((256, 6 * TRACE))
    pick = np.zeros((6 * TRACE, 256))
    half = 0.5 * END_LIFT
    for a in range(3):
        va = 64 * (1 + a)
        own[:64, va : va + 64] -= along(deriv, a)
        own[va : va + 64, :64] -= along(deriv, a)
        others = [64 * (1 + b) for b in range(3) if b != a]
        for side in range(2):
            face = 2 * a + side
            sign = 2.0 * side - 1.0
            for number, n in enumerate(face_nodes(a, side)):
                own[n, n] -= half
                own[n, va + n] += half * sign
                own[va + n, va + n] -= half
                own[va + n, n] += half * sign
                at = TRACE * face + number
                lift[n, at] = half
                lift[va + n, at] = -half * sign
                pick[at, n] = 1.0
                pick[at, va + n] = sign
                for place, row in enumerate(others):
                    own[row + n, row + n] -= half
                    lift[row + n, at + 16 * (1 + place)] = half
                    pick[at + 16 * (1 + place), row + n] = 1.0
    diff = np.array(CELL_DIFFERENCE)
    curl = np.zeros((192, 192))
    for a in range(3):
        b, c = (a + 1) % 3, (a + 2) % 3
        curl[64 * a : 64 * a + 64, 64 * c : 64 * c + 64] += along(diff, b)
        curl[64 * a : 64 * a + 64, 64 * b : 64 * b + 64] -= along(diff, c)
    own = own.astype(np.float32)
    own_high = own.astype(jnp.bfloat16)
    own_low = (own - own_high.astype(np.float32)).astype(jnp.bfloat16)
    return [m.astype(jnp.bfloat16) for m in (own_high, own_low, lift, pick, curl)]


def slot_number(offset):
    return offset + SPREAD if offset < 0 else offset + SPREAD - 1


def split(value):
    high = value.astype(BF16)
    return high, (value - high.astype(F32)).astype(BF16)


def dot(a, b):
    return jnp.dot(a, b, preferred_element_type=F32)


def dot_nt(a, b):
    return lax.dot_general(a, b, (((1,), (1,)), ((), ())), preferred_element_type=F32)


def ones_where(condition):
    return jnp.where(condition, 1.0, 0.0).astype(BF16)


def rows_of(shape):
    return lax.broadcasted_iota(jnp.int32, shape, 0)


def lanes_of(shape):
    return lax.broadcasted_iota(jnp.int32, shape, 1)


def kernel(
    n_sec, n_dom,
    fields, source_map, new_owner, send_list, face_slot,
    own_high, own_low, lift, pick, curl,
    out,
    carry, force, lamb, near, far, sends, row_list,
    move_out, move_in, force_out, force_in, sent, received,
    lamb_send, lamb_recv, move_send, move_recv, force_send, force_recv, face_send, face_recv,
):
    sec, me = lax.axis_index("sec"), lax.axis_index("dom")
    elements = fields.shape[1]
    blocks = new_owner.shape[1]
    flow = sec == 0
    acoustic = sec > 0
    inside = [(me + o >= 0) & (me + o < n_dom) for o in OFFSETS]

    barrier = pltpu.get_barrier_semaphore()
    greeted = jnp.where(flow, n_sec - 1, 1)
    for slot, o in enumerate(OFFSETS):
        greeted = greeted + jnp.where(inside[slot], 1, 0)

        @pl.when(inside[slot])
        def _():
            pl.semaphore_signal(barrier, inc=1, device_id=(sec, me + o), device_id_type=MESH)

    @pl.when(flow)
    def _():
        for other in range(1, n_sec):
            pl.semaphore_signal(barrier, inc=1, device_id=(other, me), device_id_type=MESH)

    @pl.when(acoustic)
    def _():
        pl.semaphore_signal(barrier, inc=1, device_id=(0, me), device_id_type=MESH)

    def lamb_copy(chunk, other):
        part = lamb.at[pl.ds(64 * chunk, 64)]
        return pltpu.make_async_remote_copy(
            src_ref=part,
            dst_ref=part,
            send_sem=lamb_send.at[chunk, other - 1],
            recv_sem=lamb_recv.at[chunk],
            device_id=(other, me),
            device_id_type=MESH,
        )

    def peer_copy(source, target, send_sem, recv_sem, slot):
        there = PEERS - 1 - slot
        return pltpu.make_async_remote_copy(
            src_ref=source,
            dst_ref=target.at[there],
            send_sem=send_sem.at[slot],
            recv_sem=recv_sem.at[there],
            device_id=(sec, me + OFFSETS[slot]),
            device_id_type=MESH,
        )

    def start_all(copies):
        for slot in range(PEERS):

            @pl.when(inside[slot])
            def _():
                copies(slot).start()

    def wait_recv_all(target, recv_sem, send_sem):
        for slot in range(PEERS):

            @pl.when(inside[slot])
            def _():
                pltpu.make_async_remote_copy(
                    src_ref=target.at[slot],
                    dst_ref=target.at[slot],
                    send_sem=send_sem.at[slot],
                    recv_sem=recv_sem.at[slot],
                    device_id=(sec, me + OFFSETS[slot]),
                    device_id_type=MESH,
                ).wait_recv()

    def wait_send_all(copies):
        for slot in range(PEERS):

            @pl.when(inside[slot])
            def _():
                copies(slot).wait_send()

    @pl.when(flow)
    def _():
        high, low = split(fields[0:192, :])
        spin = dot(curl[...], high) + dot(curl[...], low)
        u = [fields[64 * a : 64 * a + 64, :] for a in range(3)]
        w = [spin[64 * a : 64 * a + 64, :] for a in range(3)]
        rho = fields[192:256, :]
        for a in range(3):
            b, c = (a + 1) % 3, (a + 2) % 3
            lamb[64 * a : 64 * a + 64, :] = rho * (w[b] * u[c] - w[c] * u[b])

    spread_shape = (blocks, elements)
    spread = ones_where(lanes_of(spread_shape) // BLOCK_SIZE == rows_of(spread_shape))
    owner = jnp.broadcast_to((new_owner[...] - me).astype(F32), (8, blocks)).astype(BF16)
    away = dot(owner, spread)
    group = rows_of((8, elements))
    wanted = jnp.where(group <= SPREAD, group - SPREAD - 1, group - SPREAD)
    wanted = jnp.where(group == 0, 0, jnp.where(group > PEERS, 99, wanted)).astype(F32)
    match = jnp.where(away == wanted, 1.0, 0.0)
    square = (elements, elements)
    before = ones_where(rows_of(square) < lanes_of(square))
    place = dot(match.astype(BF16), before)
    counts = jnp.sum(match, axis=1, keepdims=True)
    keep_match = jnp.where(group == 0, match, 0.0)
    move_match = match - keep_match
    base = (MOVE * (group - 1)).astype(F32)
    kept = jnp.sum(keep_match * (place + 1.0), axis=0, keepdims=True).astype(jnp.int32) - 1
    moved = jnp.sum(move_match * (place + base + 1.0), axis=0, keepdims=True).astype(jnp.int32) - 1
    total = PEERS * MOVE
    move_sel = ones_where(rows_of((total, elements)) == moved)

    field_high, field_low = split(fields[...])
    outgoing = dot_nt(move_sel, field_high) + dot_nt(move_sel, field_low)
    for slot in range(PEERS):
        move_out[slot] = outgoing[MOVE * slot : MOVE * slot + MOVE, :]

    def moves(slot):
        return peer_copy(move_out.at[slot], move_in, move_send, move_recv, slot)

    pl.semaphore_wait(barrier, greeted)
    start_all(moves)

    @pl.when(flow)
    def _():
        for chunk in range(3):
            for other in range(1, n_sec):
                lamb_copy(chunk, other).start()

    for slot in range(PEERS):

        @pl.when(jnp.logical_not(inside[slot]))
        def _():
            move_in[slot] = jnp.zeros(move_in.shape[1:], F32)
            force_in[slot] = jnp.zeros(force_in.shape[1:], F32)

    keep_sel = ones_where(rows_of(square) == kept)
    stays = dot_nt(field_high, keep_sel) + dot_nt(field_low, keep_sel)
    arrive = []
    start = counts[0:1, :]
    part_shape = (MOVE, elements)
    for slot in range(PEERS):
        number = rows_of(part_shape).astype(F32)
        count = counts[slot + 1 : slot + 2, :]
        hit = (lanes_of(part_shape).astype(F32) == start + number) & (number < count)
        arrive.append(jnp.where(hit, 1.0, 0.0))
        start = start + count
    arrive = jnp.concatenate(arrive, axis=0).astype(BF16)

    def arrived(ref):
        rows = jnp.concatenate([ref[slot] for slot in range(PEERS)], axis=0)
        high, low = split(rows.T)
        return dot(high, arrive) + dot(low, arrive)

    @pl.when(acoustic)
    def _():
        row_list[...] = jnp.full(row_list.shape, -1, jnp.int32)
        row_list[:, 0 : PEERS * FACE_CAP] = send_list[...]
        lane = rows_of((LANES, elements))
        entry = (PEERS - 1 - lane // FACE_CAP) * FACE_CAP + lane % FACE_CAP
        entry = jnp.where(lane < PEERS * FACE_CAP, entry + 6 * elements, -7)
        for face in range(6):
            slots = face_slot[face : face + 1, :]
            near[face] = ones_where(rows_of(square) + (face ^ 1) * elements == slots)
            far[:, elements * face : elements * face + elements] = ones_where(entry == slots)
            shape = (elements, LANES)
            sends[elements * face : elements * face + elements, :] = ones_where(
                rows_of(shape) + face * elements == row_list[...]
            )

    wait_recv_all(move_in, move_recv, move_send)
    out[...] = stays + arrived(move_in)

    @pl.when(acoustic)
    def _():
        lane = lanes_of((TRACE, LANES))
        for segment in range(SEGMENTS):

            def faces(slot):
                return peer_copy(
                    sent.at[segment], received.at[segment], face_send.at[segment], face_recv.at[segment], slot
                )

            high, low = split(out[...])
            shown = dot(pick[...], high) + dot(pick[...], low)
            shown_high, shown_low = split(shown)
            pairs = [
                jnp.concatenate(
                    [shown_high[TRACE * f : TRACE * f + TRACE], shown_low[TRACE * f : TRACE * f + TRACE]], axis=0
                )
                for f in range(6)
            ]
            listed = dot(jnp.concatenate(pairs, axis=1), sends[...])
            sent[segment] = listed[:TRACE] + listed[TRACE:]
            start_all(faces)
            rate = dot(own_high[...], high) + dot(own_high[...], low) + dot(own_low[...], high)
            local = [dot(pairs[f ^ 1], near[f]) for f in range(6)]
            if segment == 0:
                rows = lanes_of(square)
                source = ones_where(rows_of(square) == source_map[...])
                force_sel = dot_nt(move_sel, source).astype(BF16)
                stay_sel = dot_nt(source, keep_sel).astype(BF16)
                for chunk in range(3):
                    lamb_copy(chunk, 1).wait_recv()
                lamb_high, lamb_low = split(lamb[...])
                leaving = dot_nt(force_sel, lamb_high) + dot_nt(force_sel, lamb_low)
                for slot in range(PEERS):
                    force_out[slot] = leaving[MOVE * slot : MOVE * slot + MOVE, :]

                def forces(slot):
                    return peer_copy(force_out.at[slot], force_in, force_send, force_recv, slot)

                start_all(forces)
                stays_force = dot(lamb_high, stay_sel) + dot(lamb_low, stay_sel)
                wait_recv_all(force_in, force_recv, force_send)
                force[...] = stays_force + arrived(force_in)
            wait_recv_all(received.at[segment], face_recv.at[segment], face_send.at[segment])
            merged = jnp.zeros((TRACE, LANES), F32)
            for slot in range(PEERS):
                first = (PEERS - 1 - slot) * FACE_CAP
                here = (lane >= first) & (lane < first + FACE_CAP) & inside[slot]
                merged = jnp.where(here, received[segment, slot], merged)
            merged_high, merged_low = split(merged)
            remote = dot(jnp.concatenate([merged_high, merged_low], axis=0), far[...])
            outside = [local[f] + remote[:, elements * f : elements * f + elements] for f in range(6)]
            outside_high = jnp.concatenate([piece[:TRACE] for piece in outside], axis=0).astype(BF16)
            outside_low = jnp.concatenate([piece[TRACE:] for piece in outside], axis=0).astype(BF16)
            rate = rate + dot(lift[...], outside_high) + dot(lift[...], outside_low)
            rate = jnp.concatenate([rate[:64], rate[64:] + force[...]], axis=0)
            now = TIME_STEP * rate
            if segment > 0:
                now = SEGMENT_CARRY[segment] * carry[...] + now
            carry[...] = now
            out[...] = out[...] + SEGMENT_WEIGHTS[segment] * now

        for segment in range(SEGMENTS):
            wait_send_all(
                lambda slot: peer_copy(
                    sent.at[segment], received.at[segment], face_send.at[segment], face_recv.at[segment], slot
                )
            )
        wait_send_all(lambda slot: peer_copy(force_out.at[slot], force_in, force_send, force_recv, slot))

    wait_send_all(moves)

    @pl.when(flow)
    def _():
        for chunk in range(3):
            for other in range(1, n_sec):
                lamb_copy(chunk, other).wait_send()


def local(n_sec, n_dom, fields, source_map, new_owner, send_list, face_slot):
    rows = fields.shape[0] * fields.shape[1]
    elements = fields.shape[2]
    dma = pltpu.SemaphoreType.DMA
    vmem = pltpu.VMEM
    consts = [jnp.asarray(m) for m in constants()]
    call = pl.pallas_call(
        functools.partial(kernel, n_sec, n_dom),
        out_shape=jax.ShapeDtypeStruct((rows, elements), F32),
        in_specs=[pl.BlockSpec(memory_space=pltpu.VMEM)] * 10,
        out_specs=pl.BlockSpec(memory_space=pltpu.VMEM),
        scratch_shapes=[
            vmem((rows, elements), F32),
            vmem((192, elements), F32),
            vmem((192, elements), F32),
            vmem((6, elements, elements), BF16),
            vmem((LANES, 6 * elements), BF16),
            vmem((6 * elements, LANES), BF16),
            vmem((1, LANES), jnp.int32),
            vmem((PEERS, MOVE, rows), F32),
            vmem((PEERS, MOVE, rows), F32),
            vmem((PEERS, MOVE, 192), F32),
            vmem((PEERS, MOVE, 192), F32),
            vmem((SEGMENTS, TRACE, LANES), F32),
            vmem((SEGMENTS, PEERS, TRACE, LANES), F32),
            dma((3, n_sec - 1)),
            dma((3,)),
            dma((PEERS,)),
            dma((PEERS,)),
            dma((PEERS,)),
            dma((PEERS,)),
            dma((SEGMENTS, PEERS)),
            dma((SEGMENTS, PEERS)),
        ],
        compiler_params=pltpu.CompilerParams(
            collective_id=0, has_side_effects=True, vmem_limit_bytes=48 * 2**20
        ),
        name="step",
    )
    made = call(
        fields.reshape(rows, elements),
        source_map.reshape(1, -1),
        new_owner.reshape(1, -1),
        send_list.reshape(1, -1),
        face_slot,
        *consts,
    )
    return made.reshape(fields.shape)


def solution(mesh):
    both = ("sec", "dom")
    in_specs = (P(None, None, both), P(both), P(both), P(both), P(None, both))
    run = functools.partial(local, mesh.shape["sec"], mesh.shape["dom"])
    return jax.shard_map(
        run, mesh=mesh, in_specs=in_specs, out_specs=P(None, None, both), check_vma=False
    )
```

```python
import functools

import jax
import jax.numpy as jnp
import numpy as np
from jax import lax
from jax.experimental import pallas as pl
from jax.experimental.pallas import tpu as pltpu
from jax.sharding import PartitionSpec as P

BLOCK_SIZE = 4
MOVE_CAP = 4
SPREAD = 2
FACE_CAP = 24
MOVE = MOVE_CAP * BLOCK_SIZE
PEERS = 2 * SPREAD
LANES = 128
TRACE = 48
SHOWN = 6 * TRACE
OFFSETS = [value for value in range(-SPREAD, SPREAD + 1) if value != 0]

CELL_DIFFERENCE = [
    [-1.0, 1.0, 0.0, 0.0],
    [-0.5, 0.0, 0.5, 0.0],
    [0.0, -0.5, 0.0, 0.5],
    [0.0, 0.0, -1.0, 1.0],
]
SEGMENT_CARRY = [
    0.0,
    -567301805773.0 / 1357537059087.0,
    -2404267990393.0 / 2016746695238.0,
    -3550918686646.0 / 2091501179385.0,
    -1275806237668.0 / 842570457699.0,
]
SEGMENT_WEIGHTS = [
    1432997174477.0 / 9575080441755.0,
    5161836677717.0 / 13612068292357.0,
    1720146321549.0 / 2090206949498.0,
    3134564353537.0 / 4481467310338.0,
    2277821191437.0 / 14882151754819.0,
]
SEGMENTS = len(SEGMENT_CARRY)
TIME_STEP = 0.12
END_LIFT = 6.0
F32 = jnp.float32
BF16 = jnp.bfloat16
MESH = pl.DeviceIdType.MESH
INPUTS = 10
CHUNKS = 4
CHUNK_ROWS = 192 // CHUNKS
FETCH_ORDER = (0, 2, 9, 1, 3, 4, 8, 5, 6, 7)


def node_derivative():
    points = np.array([-1.0, -1.0 / np.sqrt(5.0), 1.0 / np.sqrt(5.0), 1.0])
    products = np.array(
        [np.prod([points[row] - points[col] for col in range(4) if col != row]) for row in range(4)]
    )
    matrix = np.zeros((4, 4))
    for row in range(4):
        for col in range(4):
            if row != col:
                matrix[row, col] = products[row] / (products[col] * (points[row] - points[col]))
        matrix[row, row] = -np.sum(matrix[row])
    return matrix


def along(matrix, direction):
    parts = [np.eye(4)] * 3
    parts[direction] = matrix
    return np.kron(np.kron(parts[0], parts[1]), parts[2])


def face_nodes(direction, side):
    cube = np.arange(64).reshape(4, 4, 4)
    return np.take(cube, 3 * side, axis=direction).reshape(-1)


def constants():
    deriv = node_derivative()
    own = np.zeros((256, 256))
    lift = np.zeros((256, 6 * TRACE))
    pick = np.zeros((6 * TRACE, 256))
    half = 0.5 * END_LIFT
    for a in range(3):
        va = 64 * (1 + a)
        own[:64, va : va + 64] -= along(deriv, a)
        own[va : va + 64, :64] -= along(deriv, a)
        others = [64 * (1 + b) for b in range(3) if b != a]
        for side in range(2):
            face = 2 * a + side
            sign = 2.0 * side - 1.0
            for number, n in enumerate(face_nodes(a, side)):
                own[n, n] -= half
                own[n, va + n] += half * sign
                own[va + n, va + n] -= half
                own[va + n, n] += half * sign
                at = TRACE * face + number
                lift[n, at] = half
                lift[va + n, at] = -half * sign
                pick[at, n] = 1.0
                pick[at, va + n] = sign
                for place, row in enumerate(others):
                    own[row + n, row + n] -= half
                    lift[row + n, at + 16 * (1 + place)] = half
                    pick[at + 16 * (1 + place), row + n] = 1.0
    diff = np.array(CELL_DIFFERENCE)
    curl = np.zeros((192, 192))
    for a in range(3):
        b, c = (a + 1) % 3, (a + 2) % 3
        curl[64 * a : 64 * a + 64, 64 * c : 64 * c + 64] += along(diff, b)
        curl[64 * a : 64 * a + 64, 64 * b : 64 * b + 64] -= along(diff, c)
    own = np.concatenate([pick @ own, own]).astype(np.float32)
    lift = np.concatenate([pick @ lift, lift])
    own_high = own.astype(jnp.bfloat16)
    own_low = (own - own_high.astype(np.float32)).astype(jnp.bfloat16)
    return [m.astype(jnp.bfloat16) for m in (own_high, own_low, lift, pick, curl)]


def lamb_routes(n_sec):
    half = CHUNKS // 2
    if n_sec < 4:
        return [(0, other, chunk) for chunk in range(CHUNKS) for other in range(1, n_sec)]
    last = n_sec - 1
    routes = []
    for chunk in range(CHUNKS):
        for other in range(1, last):
            routes.append((0, other, (chunk + half * (other - 1)) % CHUNKS))
    for chunk in range(CHUNKS):
        routes.append((1 if chunk < half else 2, last, chunk))
    return routes


def split(value):
    high = value.astype(BF16)
    return high, (value - high.astype(F32)).astype(BF16)


def dot(a, b):
    return jnp.dot(a, b, preferred_element_type=F32)


def dot_nt(a, b):
    return lax.dot_general(a, b, (((1,), (1,)), ((), ())), preferred_element_type=F32)


def ones_where(condition):
    return jnp.where(condition, 1.0, 0.0).astype(BF16)


def rows_of(shape):
    return lax.broadcasted_iota(jnp.int32, shape, 0)


def lanes_of(shape):
    return lax.broadcasted_iota(jnp.int32, shape, 1)


def kernel(
    n_sec, n_dom,
    *refs,
):
    given, out, held = refs[:INPUTS], refs[INPUTS], refs[INPUTS + 1 : 2 * INPUTS + 1]
    fields, source_map, new_owner, send_list, face_slot, own_high, own_low, lift, pick, curl = held
    (
        carry, force, shown, shown_carry, lamb, near, far, sends, row_list,
        move_out, move_in, force_out, force_in, sent, received, in_sem,
        lamb_send, lamb_recv, move_send, move_recv, force_send, force_recv, face_send, face_recv,
    ) = refs[2 * INPUTS + 1 :]
    fetch = [pltpu.make_async_copy(given[n], held[n], in_sem.at[n]) for n in range(INPUTS)]
    for n in FETCH_ORDER:
        fetch[n].start()
    sec, me = lax.axis_index("sec"), lax.axis_index("dom")
    elements = fields.shape[1]
    blocks = new_owner.shape[1]
    flow = sec == 0
    acoustic = sec > 0
    inside = [(me + o >= 0) & (me + o < n_dom) for o in OFFSETS]

    barrier = pltpu.get_barrier_semaphore()
    routes = lamb_routes(n_sec)
    partners = {this: set() for this in range(n_sec)}
    for source, target, chunk in routes:
        partners[source].add(target)
        partners[target].add(source)
    greeted = 0
    for this in range(n_sec):
        greeted = greeted + jnp.where(sec == this, len(partners[this]), 0)
    for slot, o in enumerate(OFFSETS):
        greeted = greeted + jnp.where(inside[slot], 1, 0)

        @pl.when(inside[slot])
        def _():
            pl.semaphore_signal(barrier, inc=1, device_id=(sec, me + o), device_id_type=MESH)

    for this in range(n_sec):

        @pl.when(sec == this)
        def _():
            for other in sorted(partners[this]):
                pl.semaphore_signal(barrier, inc=1, device_id=(other, me), device_id_type=MESH)

    def lamb_copy(chunk, other):
        part = lamb.at[pl.ds(CHUNK_ROWS * chunk, CHUNK_ROWS)]
        return pltpu.make_async_remote_copy(
            src_ref=part,
            dst_ref=part,
            send_sem=lamb_send.at[chunk, other],
            recv_sem=lamb_recv.at[chunk],
            device_id=(other, me),
            device_id_type=MESH,
        )

    def peer_copy(source, target, send_sem, recv_sem, slot):
        there = PEERS - 1 - slot
        return pltpu.make_async_remote_copy(
            src_ref=source,
            dst_ref=target.at[there],
            send_sem=send_sem.at[slot],
            recv_sem=recv_sem.at[there],
            device_id=(sec, me + OFFSETS[slot]),
            device_id_type=MESH,
        )

    def start_all(copies):
        for slot in range(PEERS):

            @pl.when(inside[slot])
            def _():
                copies(slot).start()

    def wait_recv_all(target, recv_sem, send_sem):
        for slot in range(PEERS):

            @pl.when(inside[slot])
            def _():
                pltpu.make_async_remote_copy(
                    src_ref=target.at[slot],
                    dst_ref=target.at[slot],
                    send_sem=send_sem.at[slot],
                    recv_sem=recv_sem.at[slot],
                    device_id=(sec, me + OFFSETS[slot]),
                    device_id_type=MESH,
                ).wait_recv()

    def wait_send_all(copies):
        for slot in range(PEERS):

            @pl.when(inside[slot])
            def _():
                copies(slot).wait_send()

    for n in range(INPUTS):
        fetch[n].wait()

    @pl.when(flow)
    def _():
        high, low = split(fields[0:192, :])
        spin = dot(curl[...], high) + dot(curl[...], low)
        u = [fields[64 * a : 64 * a + 64, :] for a in range(3)]
        w = [spin[64 * a : 64 * a + 64, :] for a in range(3)]
        rho = fields[192:256, :]
        for a in range(3):
            b, c = (a + 1) % 3, (a + 2) % 3
            lamb[64 * a : 64 * a + 64, :] = rho * (w[b] * u[c] - w[c] * u[b])

    spread_shape = (blocks, elements)
    spread = ones_where(lanes_of(spread_shape) // BLOCK_SIZE == rows_of(spread_shape))
    owner = jnp.broadcast_to((new_owner[...] - me).astype(F32), (8, blocks)).astype(BF16)
    away = dot(owner, spread)
    group = rows_of((8, elements))
    wanted = jnp.where(group <= SPREAD, group - SPREAD - 1, group - SPREAD)
    wanted = jnp.where(group == 0, 0, jnp.where(group > PEERS, 99, wanted)).astype(F32)
    match = jnp.where(away == wanted, 1.0, 0.0)
    square = (elements, elements)
    before = ones_where(rows_of(square) < lanes_of(square))
    place = dot(match.astype(BF16), before)
    counts = jnp.sum(match, axis=1, keepdims=True)
    keep_match = jnp.where(group == 0, match, 0.0)
    move_match = match - keep_match
    base = (MOVE * (group - 1)).astype(F32)
    kept = jnp.sum(keep_match * (place + 1.0), axis=0, keepdims=True).astype(jnp.int32) - 1
    moved = jnp.sum(move_match * (place + base + 1.0), axis=0, keepdims=True).astype(jnp.int32) - 1
    total = PEERS * MOVE
    move_sel = ones_where(rows_of((total, elements)) == moved)

    field_high, field_low = split(fields[...])
    outgoing = dot_nt(move_sel, field_high) + dot_nt(move_sel, field_low)
    for slot in range(PEERS):
        move_out[slot] = outgoing[MOVE * slot : MOVE * slot + MOVE, :]

    def moves(slot):
        return peer_copy(move_out.at[slot], move_in, move_send, move_recv, slot)

    pl.semaphore_wait(barrier, greeted)
    @pl.when(flow)
    def _():
        for source, target, chunk in routes:
            if source == 0:
                lamb_copy(chunk, target).start()

    start_all(moves)

    for slot in range(PEERS):

        @pl.when(jnp.logical_not(inside[slot]))
        def _():
            move_in[slot] = jnp.zeros(move_in.shape[1:], F32)
            force_in[slot] = jnp.zeros(force_in.shape[1:], F32)

    keep_sel = ones_where(rows_of(square) == kept)
    stays = dot_nt(field_high, keep_sel) + dot_nt(field_low, keep_sel)
    arrive = []
    start = counts[0:1, :]
    part_shape = (MOVE, elements)
    for slot in range(PEERS):
        number = rows_of(part_shape).astype(F32)
        count = counts[slot + 1 : slot + 2, :]
        hit = (lanes_of(part_shape).astype(F32) == start + number) & (number < count)
        arrive.append(jnp.where(hit, 1.0, 0.0))
        start = start + count
    arrive = jnp.concatenate(arrive, axis=0).astype(BF16)

    def arrived(ref):
        rows = jnp.concatenate([ref[slot] for slot in range(PEERS)], axis=0)
        high, low = split(rows.T)
        return dot(high, arrive) + dot(low, arrive)

    @pl.when(acoustic)
    def _():
        row_list[...] = jnp.full(row_list.shape, -1, jnp.int32)
        row_list[:, 0 : PEERS * FACE_CAP] = send_list[...]
        lane = rows_of((LANES, elements))
        entry = (PEERS - 1 - lane // FACE_CAP) * FACE_CAP + lane % FACE_CAP
        entry = jnp.where(lane < PEERS * FACE_CAP, entry + 6 * elements, -7)
        for face in range(6):
            slots = face_slot[face : face + 1, :]
            near[face] = ones_where(rows_of(square) + (face ^ 1) * elements == slots)
            far[:, elements * face : elements * face + elements] = ones_where(entry == slots)
            shape = (elements, LANES)
            sends[elements * face : elements * face + elements, :] = ones_where(
                rows_of(shape) + face * elements == row_list[...]
            )

    relayed = {this: [(t, c) for source, t, c in routes if source == this] for this in range(1, n_sec)}
    for this in range(1, n_sec):
        if relayed[this]:

            @pl.when(sec == this)
            def _():
                for target, chunk in relayed[this]:
                    lamb_copy(chunk, target).wait_recv()
                    lamb_copy(chunk, target).start()

    wait_recv_all(move_in, move_recv, move_send)
    out[...] = stays + arrived(move_in)

    @pl.when(acoustic)
    def _():
        lane = lanes_of((TRACE, LANES))
        for segment in range(SEGMENTS):

            def faces(slot):
                return peer_copy(
                    sent.at[segment], received.at[segment], face_send.at[segment], face_recv.at[segment], slot
                )

            if segment == 0:
                high, low = split(out[...])
                shown[...] = dot(pick[...], high) + dot(pick[...], low)
            shown_high, shown_low = split(shown[...])
            pairs = [
                jnp.concatenate(
                    [shown_high[TRACE * f : TRACE * f + TRACE], shown_low[TRACE * f : TRACE * f + TRACE]], axis=0
                )
                for f in range(6)
            ]
            listed = dot(jnp.concatenate(pairs, axis=1), sends[...])
            sent[segment] = listed[:TRACE] + listed[TRACE:]
            start_all(faces)
            if segment > 0:
                advance(segment - 1)
                high, low = split(out[...])
            beside = [dot(pairs[f ^ 1], near[f]) for f in range(6)]
            beside_high = jnp.concatenate([piece[:TRACE] for piece in beside], axis=0).astype(BF16)
            beside_low = jnp.concatenate([piece[TRACE:] for piece in beside], axis=0).astype(BF16)
            rate = dot(own_high[...], high) + dot(own_high[...], low) + dot(own_low[...], high)
            rate = rate + dot(lift[...], beside_high) + dot(lift[...], beside_low)
            if segment == 0:
                source = ones_where(rows_of(square) == source_map[...])
                force_sel = dot_nt(move_sel, source).astype(BF16)
                stay_sel = dot_nt(source, keep_sel).astype(BF16)
                for this in range(1, n_sec):

                    @pl.when(sec == this)
                    def _():
                        early = [chunk for _, chunk in relayed[this]]
                        for chunk in range(CHUNKS):
                            if chunk not in early:
                                lamb_copy(chunk, 0).wait_recv()

                lamb_high, lamb_low = split(lamb[...])
                leaving = dot_nt(force_sel, lamb_high) + dot_nt(force_sel, lamb_low)
                for slot in range(PEERS):
                    force_out[slot] = leaving[MOVE * slot : MOVE * slot + MOVE, :]

                def forces(slot):
                    return peer_copy(force_out.at[slot], force_in, force_send, force_recv, slot)

                start_all(forces)
                stays_force = dot(lamb_high, stay_sel) + dot(lamb_low, stay_sel)
                wait_recv_all(force_in, force_recv, force_send)
                forced = stays_force + arrived(force_in)
                forced_high, forced_low = split(forced)
                force[SHOWN:, :] = forced
                force[:SHOWN, :] = dot(pick[:, 64:], forced_high) + dot(pick[:, 64:], forced_low)
            wait_recv_all(received.at[segment], face_recv.at[segment], face_send.at[segment])
            merged = jnp.zeros((TRACE, LANES), F32)
            for slot in range(PEERS):
                first = (PEERS - 1 - slot) * FACE_CAP
                here = (lane >= first) & (lane < first + FACE_CAP) & inside[slot]
                merged = jnp.where(here, received[segment, slot], merged)
            merged_high, merged_low = split(merged)
            remote = dot(jnp.concatenate([merged_high, merged_low], axis=0), far[...])
            remote = [remote[:, elements * f : elements * f + elements] for f in range(6)]
            remote_high = jnp.concatenate([piece[:TRACE] for piece in remote], axis=0).astype(BF16)
            remote_low = jnp.concatenate([piece[TRACE:] for piece in remote], axis=0).astype(BF16)
            if segment < SEGMENTS - 1:
                seen = rate[:SHOWN] + force[:SHOWN, :]
                seen = seen + dot(lift[:SHOWN, :], remote_high) + dot(lift[:SHOWN, :], remote_low)
                now = TIME_STEP * seen
                if segment > 0:
                    now = SEGMENT_CARRY[segment] * shown_carry[...] + now
                shown_carry[...] = now
                shown[...] = shown[...] + SEGMENT_WEIGHTS[segment] * now

            def advance(number, rate=rate, remote_high=remote_high, remote_low=remote_low):
                gain = rate[SHOWN:] + dot(lift[SHOWN:, :], remote_high) + dot(lift[SHOWN:, :], remote_low)
                gain = jnp.concatenate([gain[:64], gain[64:] + force[SHOWN:, :]], axis=0)
                step = TIME_STEP * gain
                if number > 0:
                    step = SEGMENT_CARRY[number] * carry[...] + step
                carry[...] = step
                out[...] = out[...] + SEGMENT_WEIGHTS[number] * step

        advance(SEGMENTS - 1)

        for segment in range(SEGMENTS):
            wait_send_all(
                lambda slot: peer_copy(
                    sent.at[segment], received.at[segment], face_send.at[segment], face_recv.at[segment], slot
                )
            )
        wait_send_all(lambda slot: peer_copy(force_out.at[slot], force_in, force_send, force_recv, slot))

    wait_send_all(moves)

    for this in range(n_sec):

        @pl.when(sec == this)
        def _():
            for source, target, chunk in routes:
                if source == this:
                    lamb_copy(chunk, target).wait_send()


def local(n_sec, n_dom, fields, source_map, new_owner, send_list, face_slot):
    rows = fields.shape[0] * fields.shape[1]
    elements = fields.shape[2]
    dma = pltpu.SemaphoreType.DMA
    vmem = pltpu.VMEM
    consts = [jnp.asarray(m) for m in constants()]
    operands = [
        fields.reshape(rows, elements),
        source_map.reshape(1, -1),
        new_owner.reshape(1, -1),
        send_list.reshape(1, -1),
        face_slot,
        *consts,
    ]
    call = pl.pallas_call(
        functools.partial(kernel, n_sec, n_dom),
        out_shape=jax.ShapeDtypeStruct((rows, elements), F32),
        in_specs=[pl.BlockSpec(memory_space=pltpu.HBM)] * INPUTS,
        out_specs=pl.BlockSpec(memory_space=pltpu.VMEM),
        scratch_shapes=[
            *[vmem(value.shape, value.dtype) for value in operands],
            vmem((rows, elements), F32),
            vmem((SHOWN + 192, elements), F32),
            vmem((SHOWN, elements), F32),
            vmem((SHOWN, elements), F32),
            vmem((192, elements), F32),
            vmem((6, elements, elements), BF16),
            vmem((LANES, 6 * elements), BF16),
            vmem((6 * elements, LANES), BF16),
            vmem((1, LANES), jnp.int32),
            vmem((PEERS, MOVE, rows), F32),
            vmem((PEERS, MOVE, rows), F32),
            vmem((PEERS, MOVE, 192), F32),
            vmem((PEERS, MOVE, 192), F32),
            vmem((SEGMENTS, TRACE, LANES), F32),
            vmem((SEGMENTS, PEERS, TRACE, LANES), F32),
            dma((INPUTS,)),
            dma((CHUNKS, n_sec)),
            dma((CHUNKS,)),
            dma((PEERS,)),
            dma((PEERS,)),
            dma((PEERS,)),
            dma((PEERS,)),
            dma((SEGMENTS, PEERS)),
            dma((SEGMENTS, PEERS)),
        ],
        compiler_params=pltpu.CompilerParams(
            collective_id=0, has_side_effects=True, vmem_limit_bytes=63 * 2**20
        ),
        name="step",
    )
    made = call(*operands)
    return made.reshape(fields.shape)


def solution(mesh):
    both = ("sec", "dom")
    in_specs = (P(None, None, both), P(both), P(both), P(both), P(None, both))
    run = functools.partial(local, mesh.shape["sec"], mesh.shape["dom"])
    return jax.shard_map(
        run, mesh=mesh, in_specs=in_specs, out_specs=P(None, None, both), check_vma=False
    )
```

```python
import functools

import jax
import jax.numpy as jnp
import numpy as np
from jax import lax
from jax.experimental import pallas as pl
from jax.experimental.pallas import tpu as pltpu
from jax.sharding import PartitionSpec as P

BLOCK_SIZE = 4
MOVE_CAP = 4
SPREAD = 2
FACE_CAP = 24
MOVE = MOVE_CAP * BLOCK_SIZE
PEERS = 2 * SPREAD
LANES = 128
TRACE = 48
SHOWN = 6 * TRACE
OFFSETS = [value for value in range(-SPREAD, SPREAD + 1) if value != 0]

CELL_DIFFERENCE = [
    [-1.0, 1.0, 0.0, 0.0],
    [-0.5, 0.0, 0.5, 0.0],
    [0.0, -0.5, 0.0, 0.5],
    [0.0, 0.0, -1.0, 1.0],
]
SEGMENT_CARRY = [
    0.0,
    -567301805773.0 / 1357537059087.0,
    -2404267990393.0 / 2016746695238.0,
    -3550918686646.0 / 2091501179385.0,
    -1275806237668.0 / 842570457699.0,
]
SEGMENT_WEIGHTS = [
    1432997174477.0 / 9575080441755.0,
    5161836677717.0 / 13612068292357.0,
    1720146321549.0 / 2090206949498.0,
    3134564353537.0 / 4481467310338.0,
    2277821191437.0 / 14882151754819.0,
]
SEGMENTS = len(SEGMENT_CARRY)
TIME_STEP = 0.12
END_LIFT = 6.0
F32 = jnp.float32
BF16 = jnp.bfloat16
MESH = pl.DeviceIdType.MESH
INPUTS = 10
CHUNKS = 4
CHUNK_ROWS = 192 // CHUNKS
FETCH_ORDER = (0, 9, 2, 3, 4, 1, 8, 5, 6, 7)


def node_derivative():
    points = np.array([-1.0, -1.0 / np.sqrt(5.0), 1.0 / np.sqrt(5.0), 1.0])
    products = np.array(
        [np.prod([points[row] - points[col] for col in range(4) if col != row]) for row in range(4)]
    )
    matrix = np.zeros((4, 4))
    for row in range(4):
        for col in range(4):
            if row != col:
                matrix[row, col] = products[row] / (products[col] * (points[row] - points[col]))
        matrix[row, row] = -np.sum(matrix[row])
    return matrix


def along(matrix, direction):
    parts = [np.eye(4)] * 3
    parts[direction] = matrix
    return np.kron(np.kron(parts[0], parts[1]), parts[2])


def face_nodes(direction, side):
    cube = np.arange(64).reshape(4, 4, 4)
    return np.take(cube, 3 * side, axis=direction).reshape(-1)


def constants():
    deriv = node_derivative()
    own = np.zeros((256, 256))
    lift = np.zeros((256, 6 * TRACE))
    pick = np.zeros((6 * TRACE, 256))
    half = 0.5 * END_LIFT
    for a in range(3):
        va = 64 * (1 + a)
        own[:64, va : va + 64] -= along(deriv, a)
        own[va : va + 64, :64] -= along(deriv, a)
        others = [64 * (1 + b) for b in range(3) if b != a]
        for side in range(2):
            face = 2 * a + side
            sign = 2.0 * side - 1.0
            for number, n in enumerate(face_nodes(a, side)):
                own[n, n] -= half
                own[n, va + n] += half * sign
                own[va + n, va + n] -= half
                own[va + n, n] += half * sign
                at = TRACE * face + number
                lift[n, at] = half
                lift[va + n, at] = -half * sign
                pick[at, n] = 1.0
                pick[at, va + n] = sign
                for place, row in enumerate(others):
                    own[row + n, row + n] -= half
                    lift[row + n, at + 16 * (1 + place)] = half
                    pick[at + 16 * (1 + place), row + n] = 1.0
    diff = np.array(CELL_DIFFERENCE)
    curl = np.zeros((192, 192))
    for a in range(3):
        b, c = (a + 1) % 3, (a + 2) % 3
        curl[64 * a : 64 * a + 64, 64 * c : 64 * c + 64] += along(diff, b)
        curl[64 * a : 64 * a + 64, 64 * b : 64 * b + 64] -= along(diff, c)
    own = np.concatenate([pick @ own, own]).astype(np.float32)
    lift = np.concatenate([pick @ lift, lift])
    lift = np.repeat(lift.reshape(-1, 6, 1, TRACE), 2, axis=2).reshape(-1, 2 * 6 * TRACE)
    own_high = own.astype(jnp.bfloat16)
    own_low = (own - own_high.astype(np.float32)).astype(jnp.bfloat16)
    return [m.astype(jnp.bfloat16) for m in (own_high, own_low, lift, pick, curl)]


def lamb_routes(n_sec):
    half = CHUNKS // 2
    if n_sec < 4:
        return [(0, other, chunk) for chunk in range(CHUNKS) for other in range(1, n_sec)]
    last = n_sec - 1
    routes = []
    for chunk in range(CHUNKS):
        for other in range(1, last):
            routes.append((0, other, (chunk + half * (other - 1)) % CHUNKS))
    for chunk in range(CHUNKS):
        routes.append((1 if chunk < half else 2, last, chunk))
    return routes


def split(value):
    high = value.astype(BF16)
    return high, (value - high.astype(F32)).astype(BF16)


def dot(a, b):
    return jnp.dot(a, b, preferred_element_type=F32)


def dot_nt(a, b):
    return lax.dot_general(a, b, (((1,), (1,)), ((), ())), preferred_element_type=F32)


def ones_where(condition):
    return jnp.where(condition, 1.0, 0.0).astype(BF16)


def rows_of(shape):
    return lax.broadcasted_iota(jnp.int32, shape, 0)


def lanes_of(shape):
    return lax.broadcasted_iota(jnp.int32, shape, 1)


def kernel(
    n_sec, n_dom,
    *refs,
):
    given, out, held = refs[:INPUTS], refs[INPUTS], refs[INPUTS + 1 : 2 * INPUTS + 1]
    fields, source_map, new_owner, send_list, face_slot, own_high, own_low, lift, pick, curl = held
    (
        carry, force, shown, shown_carry, lamb, near, far, sends, row_list,
        move_out, move_in, force_out, force_in, sent, received, in_sem,
        lamb_send, lamb_recv, move_send, move_recv, force_send, force_recv, face_send, face_recv,
    ) = refs[2 * INPUTS + 1 :]
    fetch = [pltpu.make_async_copy(given[n], held[n], in_sem.at[n]) for n in range(INPUTS)]
    for n in FETCH_ORDER:
        fetch[n].start()
    sec, me = lax.axis_index("sec"), lax.axis_index("dom")
    elements = fields.shape[1]
    blocks = new_owner.shape[1]
    flow = sec == 0
    acoustic = sec > 0
    inside = [(me + o >= 0) & (me + o < n_dom) for o in OFFSETS]

    barrier = pltpu.get_barrier_semaphore()
    routes = lamb_routes(n_sec)
    partners = {this: set() for this in range(n_sec)}
    for source, target, chunk in routes:
        partners[source].add(target)
        partners[target].add(source)
    greeted = 0
    for this in range(n_sec):
        greeted = greeted + jnp.where(sec == this, len(partners[this]), 0)
    for slot, o in enumerate(OFFSETS):
        greeted = greeted + jnp.where(inside[slot], 1, 0)

        @pl.when(inside[slot])
        def _():
            pl.semaphore_signal(barrier, inc=1, device_id=(sec, me + o), device_id_type=MESH)

    for this in range(n_sec):

        @pl.when(sec == this)
        def _():
            for other in sorted(partners[this]):
                pl.semaphore_signal(barrier, inc=1, device_id=(other, me), device_id_type=MESH)

    def lamb_copy(chunk, other):
        part = lamb.at[pl.ds(CHUNK_ROWS * chunk, CHUNK_ROWS)]
        return pltpu.make_async_remote_copy(
            src_ref=part,
            dst_ref=part,
            send_sem=lamb_send.at[chunk, other],
            recv_sem=lamb_recv.at[chunk],
            device_id=(other, me),
            device_id_type=MESH,
        )

    def peer_copy(source, target, send_sem, recv_sem, slot):
        there = PEERS - 1 - slot
        return pltpu.make_async_remote_copy(
            src_ref=source,
            dst_ref=target.at[there],
            send_sem=send_sem.at[slot],
            recv_sem=recv_sem.at[there],
            device_id=(sec, me + OFFSETS[slot]),
            device_id_type=MESH,
        )

    def start_all(copies):
        for slot in range(PEERS):

            @pl.when(inside[slot])
            def _():
                copies(slot).start()

    def wait_recv_all(target, recv_sem, send_sem):
        for slot in range(PEERS):

            @pl.when(inside[slot])
            def _():
                pltpu.make_async_remote_copy(
                    src_ref=target.at[slot],
                    dst_ref=target.at[slot],
                    send_sem=send_sem.at[slot],
                    recv_sem=recv_sem.at[slot],
                    device_id=(sec, me + OFFSETS[slot]),
                    device_id_type=MESH,
                ).wait_recv()

    def wait_send_all(copies):
        for slot in range(PEERS):

            @pl.when(inside[slot])
            def _():
                copies(slot).wait_send()

    fetch[0].wait()
    fetch[9].wait()

    @pl.when(flow)
    def _():
        high, low = split(fields[0:192, :])
        spin = dot(curl[...], high) + dot(curl[...], low)
        u = [fields[64 * a : 64 * a + 64, :] for a in range(3)]
        w = [spin[64 * a : 64 * a + 64, :] for a in range(3)]
        rho = fields[192:256, :]
        for a in range(3):
            b, c = (a + 1) % 3, (a + 2) % 3
            lamb[64 * a : 64 * a + 64, :] = rho * (w[b] * u[c] - w[c] * u[b])

    pl.semaphore_wait(barrier, greeted)

    @pl.when(flow)
    def _():
        for source, target, chunk in routes:
            if source == 0:
                lamb_copy(chunk, target).start()

    fetch[2].wait()
    spread_shape = (blocks, elements)
    spread = ones_where(lanes_of(spread_shape) // BLOCK_SIZE == rows_of(spread_shape))
    owner = jnp.broadcast_to((new_owner[...] - me).astype(F32), (8, blocks)).astype(BF16)
    away = dot(owner, spread)
    group = rows_of((8, elements))
    wanted = jnp.where(group <= SPREAD, group - SPREAD - 1, group - SPREAD)
    wanted = jnp.where(group == 0, 0, jnp.where(group > PEERS, 99, wanted)).astype(F32)
    match = jnp.where(away == wanted, 1.0, 0.0)
    square = (elements, elements)
    before = ones_where(rows_of(square) < lanes_of(square))
    place = dot(match.astype(BF16), before)
    counts = jnp.sum(match, axis=1, keepdims=True)
    keep_match = jnp.where(group == 0, match, 0.0)
    move_match = match - keep_match
    base = (MOVE * (group - 1)).astype(F32)
    kept = jnp.sum(keep_match * (place + 1.0), axis=0, keepdims=True).astype(jnp.int32) - 1
    moved = jnp.sum(move_match * (place + base + 1.0), axis=0, keepdims=True).astype(jnp.int32) - 1
    total = PEERS * MOVE
    move_sel = ones_where(rows_of((total, elements)) == moved)

    field_high, field_low = split(fields[...])
    outgoing = dot_nt(move_sel, field_high) + dot_nt(move_sel, field_low)
    for slot in range(PEERS):
        move_out[slot] = outgoing[MOVE * slot : MOVE * slot + MOVE, :]

    def moves(slot):
        return peer_copy(move_out.at[slot], move_in, move_send, move_recv, slot)

    start_all(moves)
    for n in (1, 3, 4, 8, 5, 6, 7):
        fetch[n].wait()

    for slot in range(PEERS):

        @pl.when(jnp.logical_not(inside[slot]))
        def _():
            move_in[slot] = jnp.zeros(move_in.shape[1:], F32)
            force_in[slot] = jnp.zeros(force_in.shape[1:], F32)

    keep_sel = ones_where(rows_of(square) == kept)
    stays = dot_nt(field_high, keep_sel) + dot_nt(field_low, keep_sel)
    arrive = []
    start = counts[0:1, :]
    part_shape = (MOVE, elements)
    for slot in range(PEERS):
        number = rows_of(part_shape).astype(F32)
        count = counts[slot + 1 : slot + 2, :]
        hit = (lanes_of(part_shape).astype(F32) == start + number) & (number < count)
        arrive.append(jnp.where(hit, 1.0, 0.0))
        start = start + count
    arrive = jnp.concatenate(arrive, axis=0).astype(BF16)

    def arrived(ref):
        rows = jnp.concatenate([ref[slot] for slot in range(PEERS)], axis=0)
        high, low = split(rows.T)
        return dot(high, arrive) + dot(low, arrive)

    @pl.when(acoustic)
    def _():
        row_list[...] = jnp.full(row_list.shape, -1, jnp.int32)
        row_list[:, 0 : PEERS * FACE_CAP] = send_list[...]
        lane = rows_of((LANES, elements))
        entry = (PEERS - 1 - lane // FACE_CAP) * FACE_CAP + lane % FACE_CAP
        entry = jnp.where(lane < PEERS * FACE_CAP, entry + 6 * elements, -7)
        for face in range(6):
            slots = face_slot[face : face + 1, :]
            near[face] = ones_where(rows_of(square) + (face ^ 1) * elements == slots)
            far[:, elements * face : elements * face + elements] = ones_where(entry == slots)
            shape = (elements, LANES)
            sends[elements * face : elements * face + elements, :] = ones_where(
                rows_of(shape) + face * elements == row_list[...]
            )

    relayed = {this: [(t, c) for source, t, c in routes if source == this] for this in range(1, n_sec)}
    for this in range(1, n_sec):
        if relayed[this]:

            @pl.when(sec == this)
            def _():
                for target, chunk in relayed[this]:
                    lamb_copy(chunk, target).wait_recv()
                    lamb_copy(chunk, target).start()

    wait_recv_all(move_in, move_recv, move_send)
    out[...] = stays + arrived(move_in)

    @pl.when(acoustic)
    def _():
        lane = lanes_of((TRACE, LANES))
        for segment in range(SEGMENTS):

            def faces(slot):
                return peer_copy(
                    sent.at[segment], received.at[segment], face_send.at[segment], face_recv.at[segment], slot
                )

            if segment == 0:
                high, low = split(out[...])
                shown[...] = dot(pick[...], high) + dot(pick[...], low)
            shown_high, shown_low = split(shown[...])
            pairs = [
                jnp.concatenate(
                    [shown_high[TRACE * f : TRACE * f + TRACE], shown_low[TRACE * f : TRACE * f + TRACE]], axis=0
                )
                for f in range(6)
            ]
            listed = dot(jnp.concatenate(pairs, axis=1), sends[...])
            sent[segment] = listed[:TRACE] + listed[TRACE:]
            start_all(faces)
            if segment > 0:
                advance(segment - 1)
                high, low = split(out[...])
            beside = [dot(pairs[f ^ 1], near[f]) for f in range(6)]
            beside_pair = jnp.concatenate(beside, axis=0).astype(BF16)
            rate = dot(own_high[...], high) + dot(own_high[...], low) + dot(own_low[...], high)
            rate = rate + dot(lift[...], beside_pair)
            if segment == 0:
                source = ones_where(rows_of(square) == source_map[...])
                force_sel = dot_nt(move_sel, source).astype(BF16)
                stay_sel = dot_nt(source, keep_sel).astype(BF16)
                for this in range(1, n_sec):

                    @pl.when(sec == this)
                    def _():
                        early = [chunk for _, chunk in relayed[this]]
                        for chunk in range(CHUNKS):
                            if chunk not in early:
                                lamb_copy(chunk, 0).wait_recv()

                lamb_high, lamb_low = split(lamb[...])
                leaving = dot_nt(force_sel, lamb_high) + dot_nt(force_sel, lamb_low)
                for slot in range(PEERS):
                    force_out[slot] = leaving[MOVE * slot : MOVE * slot + MOVE, :]

                def forces(slot):
                    return peer_copy(force_out.at[slot], force_in, force_send, force_recv, slot)

                start_all(forces)
                stays_force = dot(lamb_high, stay_sel) + dot(lamb_low, stay_sel)
                wait_recv_all(force_in, force_recv, force_send)
                forced = stays_force + arrived(force_in)
                forced_high, forced_low = split(forced)
                force[SHOWN:, :] = forced
                force[:SHOWN, :] = dot(pick[:, 64:], forced_high) + dot(pick[:, 64:], forced_low)
            wait_recv_all(received.at[segment], face_recv.at[segment], face_send.at[segment])
            merged = jnp.zeros((TRACE, LANES), F32)
            for slot in range(PEERS):
                first = (PEERS - 1 - slot) * FACE_CAP
                here = (lane >= first) & (lane < first + FACE_CAP) & inside[slot]
                merged = jnp.where(here, received[segment, slot], merged)
            merged_high, merged_low = split(merged)
            remote = dot(jnp.concatenate([merged_high, merged_low], axis=0), far[...])
            remote = [remote[:, elements * f : elements * f + elements] for f in range(6)]
            remote_pair = jnp.concatenate(remote, axis=0).astype(BF16)
            if segment < SEGMENTS - 1:
                seen = rate[:SHOWN] + force[:SHOWN, :]
                seen = seen + dot(lift[:SHOWN, :], remote_pair)
                now = TIME_STEP * seen
                if segment > 0:
                    now = SEGMENT_CARRY[segment] * shown_carry[...] + now
                shown_carry[...] = now
                shown[...] = shown[...] + SEGMENT_WEIGHTS[segment] * now

            def advance(number, rate=rate, remote_pair=remote_pair):
                gain = rate[SHOWN:] + dot(lift[SHOWN:, :], remote_pair)
                gain = jnp.concatenate([gain[:64], gain[64:] + force[SHOWN:, :]], axis=0)
                step = TIME_STEP * gain
                if number > 0:
                    step = SEGMENT_CARRY[number] * carry[...] + step
                carry[...] = step
                out[...] = out[...] + SEGMENT_WEIGHTS[number] * step

        advance(SEGMENTS - 1)

        for segment in range(SEGMENTS):
            wait_send_all(
                lambda slot: peer_copy(
                    sent.at[segment], received.at[segment], face_send.at[segment], face_recv.at[segment], slot
                )
            )
        wait_send_all(lambda slot: peer_copy(force_out.at[slot], force_in, force_send, force_recv, slot))

    wait_send_all(moves)

    for this in range(n_sec):

        @pl.when(sec == this)
        def _():
            for source, target, chunk in routes:
                if source == this:
                    lamb_copy(chunk, target).wait_send()


def local(n_sec, n_dom, fields, source_map, new_owner, send_list, face_slot):
    rows = fields.shape[0] * fields.shape[1]
    elements = fields.shape[2]
    dma = pltpu.SemaphoreType.DMA
    vmem = pltpu.VMEM
    consts = [jnp.asarray(m) for m in constants()]
    operands = [
        fields.reshape(rows, elements),
        source_map.reshape(1, -1),
        new_owner.reshape(1, -1),
        send_list.reshape(1, -1),
        face_slot,
        *consts,
    ]
    call = pl.pallas_call(
        functools.partial(kernel, n_sec, n_dom),
        out_shape=jax.ShapeDtypeStruct((rows, elements), F32),
        in_specs=[pl.BlockSpec(memory_space=pltpu.HBM)] * INPUTS,
        out_specs=pl.BlockSpec(memory_space=pltpu.VMEM),
        scratch_shapes=[
            *[vmem(value.shape, value.dtype) for value in operands],
            vmem((rows, elements), F32),
            vmem((SHOWN + 192, elements), F32),
            vmem((SHOWN, elements), F32),
            vmem((SHOWN, elements), F32),
            vmem((192, elements), F32),
            vmem((6, elements, elements), BF16),
            vmem((LANES, 6 * elements), BF16),
            vmem((6 * elements, LANES), BF16),
            vmem((1, LANES), jnp.int32),
            vmem((PEERS, MOVE, rows), F32),
            vmem((PEERS, MOVE, rows), F32),
            vmem((PEERS, MOVE, 192), F32),
            vmem((PEERS, MOVE, 192), F32),
            vmem((SEGMENTS, TRACE, LANES), F32),
            vmem((SEGMENTS, PEERS, TRACE, LANES), F32),
            dma((INPUTS,)),
            dma((CHUNKS, n_sec)),
            dma((CHUNKS,)),
            dma((PEERS,)),
            dma((PEERS,)),
            dma((PEERS,)),
            dma((PEERS,)),
            dma((SEGMENTS, PEERS)),
            dma((SEGMENTS, PEERS)),
        ],
        compiler_params=pltpu.CompilerParams(
            collective_id=0, has_side_effects=True, vmem_limit_bytes=63 * 2**20
        ),
        name="step",
    )
    made = call(*operands)
    return made.reshape(fields.shape)


def solution(mesh):
    both = ("sec", "dom")
    in_specs = (P(None, None, both), P(both), P(both), P(both), P(None, both))
    run = functools.partial(local, mesh.shape["sec"], mesh.shape["dom"])
    return jax.shard_map(
        run, mesh=mesh, in_specs=in_specs, out_specs=P(None, None, both), check_vma=False
    )
```

```python
import functools

import jax
import jax.numpy as jnp
import numpy as np
from jax import lax
from jax.experimental import pallas as pl
from jax.experimental.pallas import tpu as pltpu
from jax.sharding import PartitionSpec as P

BLOCK_SIZE = 4
MOVE_CAP = 4
SPREAD = 2
FACE_CAP = 24
MOVE = MOVE_CAP * BLOCK_SIZE
PEERS = 2 * SPREAD
LANES = 128
TRACE = 48
SHOWN = 6 * TRACE
OFFSETS = [value for value in range(-SPREAD, SPREAD + 1) if value != 0]

CELL_DIFFERENCE = [
    [-1.0, 1.0, 0.0, 0.0],
    [-0.5, 0.0, 0.5, 0.0],
    [0.0, -0.5, 0.0, 0.5],
    [0.0, 0.0, -1.0, 1.0],
]
SEGMENT_CARRY = [
    0.0,
    -567301805773.0 / 1357537059087.0,
    -2404267990393.0 / 2016746695238.0,
    -3550918686646.0 / 2091501179385.0,
    -1275806237668.0 / 842570457699.0,
]
SEGMENT_WEIGHTS = [
    1432997174477.0 / 9575080441755.0,
    5161836677717.0 / 13612068292357.0,
    1720146321549.0 / 2090206949498.0,
    3134564353537.0 / 4481467310338.0,
    2277821191437.0 / 14882151754819.0,
]
SEGMENTS = len(SEGMENT_CARRY)
TIME_STEP = 0.12
END_LIFT = 6.0
F32 = jnp.float32
BF16 = jnp.bfloat16
MESH = pl.DeviceIdType.MESH
INPUTS = 7
CHUNKS = 4
CHUNK_ROWS = 192 // CHUNKS
FETCH_ORDER = (0, 5, 2, 3, 4, 1, 6)


def node_derivative():
    points = np.array([-1.0, -1.0 / np.sqrt(5.0), 1.0 / np.sqrt(5.0), 1.0])
    products = np.array(
        [np.prod([points[row] - points[col] for col in range(4) if col != row]) for row in range(4)]
    )
    matrix = np.zeros((4, 4))
    for row in range(4):
        for col in range(4):
            if row != col:
                matrix[row, col] = products[row] / (products[col] * (points[row] - points[col]))
        matrix[row, row] = -np.sum(matrix[row])
    return matrix


def along(matrix, direction):
    parts = [np.eye(4)] * 3
    parts[direction] = matrix
    return np.kron(np.kron(parts[0], parts[1]), parts[2])


def face_nodes(direction, side):
    cube = np.arange(64).reshape(4, 4, 4)
    return np.take(cube, 3 * side, axis=direction).reshape(-1)


def constants():
    deriv = node_derivative()
    own = np.zeros((256, 256))
    lift = np.zeros((256, 6 * TRACE))
    pick = np.zeros((6 * TRACE, 256))
    half = 0.5 * END_LIFT
    for a in range(3):
        va = 64 * (1 + a)
        own[:64, va : va + 64] -= along(deriv, a)
        own[va : va + 64, :64] -= along(deriv, a)
        others = [64 * (1 + b) for b in range(3) if b != a]
        for side in range(2):
            face = 2 * a + side
            sign = 2.0 * side - 1.0
            for number, n in enumerate(face_nodes(a, side)):
                own[n, n] -= half
                own[n, va + n] += half * sign
                own[va + n, va + n] -= half
                own[va + n, n] += half * sign
                at = TRACE * face + number
                lift[n, at] = half
                lift[va + n, at] = -half * sign
                pick[at, n] = 1.0
                pick[at, va + n] = sign
                for place, row in enumerate(others):
                    own[row + n, row + n] -= half
                    lift[row + n, at + 16 * (1 + place)] = half
                    pick[at + 16 * (1 + place), row + n] = 1.0
    diff = np.array(CELL_DIFFERENCE)
    curl = np.zeros((192, 192))
    for a in range(3):
        b, c = (a + 1) % 3, (a + 2) % 3
        curl[64 * a : 64 * a + 64, 64 * c : 64 * c + 64] += along(diff, b)
        curl[64 * a : 64 * a + 64, 64 * b : 64 * b + 64] -= along(diff, c)
    own = np.concatenate([pick @ own, own]).astype(np.float32)
    lift = np.concatenate([pick @ lift, lift])
    lift = np.repeat(lift.reshape(-1, 6, 1, TRACE), 2, axis=2).reshape(-1, 2 * 6 * TRACE)
    own_high = own.astype(jnp.bfloat16)
    own_low = (own - own_high.astype(np.float32)).astype(jnp.bfloat16)
    curl = np.pad(curl, ((0, 0), (0, 256 - curl.shape[1])))
    square = np.concatenate([m.astype(jnp.bfloat16) for m in (curl, pick, own_high, own_low)])
    return [square, lift.astype(jnp.bfloat16)]


def lamb_routes(n_sec):
    half = CHUNKS // 2
    if n_sec < 4:
        return [(0, other, chunk) for chunk in range(CHUNKS) for other in range(1, n_sec)]
    last = n_sec - 1
    routes = []
    for chunk in range(CHUNKS):
        for other in range(1, last):
            routes.append((0, other, (chunk + half * (other - 1)) % CHUNKS))
    for chunk in range(CHUNKS):
        routes.append((1 if chunk < half else 2, last, chunk))
    return routes


def split(value):
    high = value.astype(BF16)
    return high, (value - high.astype(F32)).astype(BF16)


def dot(a, b):
    return jnp.dot(a, b, preferred_element_type=F32)


def dot_nt(a, b):
    return lax.dot_general(a, b, (((1,), (1,)), ((), ())), preferred_element_type=F32)


def ones_where(condition):
    return jnp.where(condition, 1.0, 0.0).astype(BF16)


def rows_of(shape):
    return lax.broadcasted_iota(jnp.int32, shape, 0)


def lanes_of(shape):
    return lax.broadcasted_iota(jnp.int32, shape, 1)


def kernel(
    n_sec, n_dom,
    *refs,
):
    given, out, held = refs[:INPUTS], refs[INPUTS], refs[INPUTS + 1 : 2 * INPUTS + 1]
    fields, source_map, new_owner, send_list, face_slot, square_parts, lift = held
    ends = (0, 192, 192 + SHOWN, 448 + 2 * SHOWN, 704 + 3 * SHOWN)
    curl, pick, own_high, own_low = [
        square_parts.at[pl.ds(ends[n], ends[n + 1] - ends[n])] for n in range(4)
    ]
    (
        carry, force, shown, shown_carry, lamb, near, far, sends, row_list,
        move_out, move_in, force_out, force_in, sent, received, in_sem,
        lamb_send, lamb_recv, move_send, move_recv, force_send, force_recv, face_send, face_recv,
    ) = refs[2 * INPUTS + 1 :]
    fetch = [pltpu.make_async_copy(given[n], held[n], in_sem.at[n]) for n in range(INPUTS)]
    for n in FETCH_ORDER:
        fetch[n].start()
    sec, me = lax.axis_index("sec"), lax.axis_index("dom")
    elements = fields.shape[1]
    blocks = new_owner.shape[1]
    flow = sec == 0
    acoustic = sec > 0
    inside = [(me + o >= 0) & (me + o < n_dom) for o in OFFSETS]

    barrier = pltpu.get_barrier_semaphore()
    routes = lamb_routes(n_sec)
    partners = {this: set() for this in range(n_sec)}
    for source, target, chunk in routes:
        partners[source].add(target)
        partners[target].add(source)
    greeted = 0
    for this in range(n_sec):
        greeted = greeted + jnp.where(sec == this, len(partners[this]), 0)
    for slot, o in enumerate(OFFSETS):
        greeted = greeted + jnp.where(inside[slot], 1, 0)

        @pl.when(inside[slot])
        def _():
            pl.semaphore_signal(barrier, inc=1, device_id=(sec, me + o), device_id_type=MESH)

    for this in range(n_sec):

        @pl.when(sec == this)
        def _():
            for other in sorted(partners[this]):
                pl.semaphore_signal(barrier, inc=1, device_id=(other, me), device_id_type=MESH)

    def lamb_copy(chunk, other):
        part = lamb.at[pl.ds(CHUNK_ROWS * chunk, CHUNK_ROWS)]
        return pltpu.make_async_remote_copy(
            src_ref=part,
            dst_ref=part,
            send_sem=lamb_send.at[chunk, other],
            recv_sem=lamb_recv.at[chunk],
            device_id=(other, me),
            device_id_type=MESH,
        )

    def peer_copy(source, target, send_sem, recv_sem, slot):
        there = PEERS - 1 - slot
        return pltpu.make_async_remote_copy(
            src_ref=source,
            dst_ref=target.at[there],
            send_sem=send_sem.at[slot],
            recv_sem=recv_sem.at[there],
            device_id=(sec, me + OFFSETS[slot]),
            device_id_type=MESH,
        )

    def start_all(copies):
        for slot in range(PEERS):

            @pl.when(inside[slot])
            def _():
                copies(slot).start()

    def wait_recv_all(target, recv_sem, send_sem):
        for slot in range(PEERS):

            @pl.when(inside[slot])
            def _():
                pltpu.make_async_remote_copy(
                    src_ref=target.at[slot],
                    dst_ref=target.at[slot],
                    send_sem=send_sem.at[slot],
                    recv_sem=recv_sem.at[slot],
                    device_id=(sec, me + OFFSETS[slot]),
                    device_id_type=MESH,
                ).wait_recv()

    def wait_send_all(copies):
        for slot in range(PEERS):

            @pl.when(inside[slot])
            def _():
                copies(slot).wait_send()

    fetch[0].wait()
    fetch[5].wait()

    @pl.when(flow)
    def _():
        high, low = split(fields[0:192, :])
        spin = dot(curl[:, :192], high) + dot(curl[:, :192], low)
        u = [fields[64 * a : 64 * a + 64, :] for a in range(3)]
        w = [spin[64 * a : 64 * a + 64, :] for a in range(3)]
        rho = fields[192:256, :]
        for a in range(3):
            b, c = (a + 1) % 3, (a + 2) % 3
            lamb[64 * a : 64 * a + 64, :] = rho * (w[b] * u[c] - w[c] * u[b])

    pl.semaphore_wait(barrier, greeted)

    @pl.when(flow)
    def _():
        for source, target, chunk in routes:
            if source == 0:
                lamb_copy(chunk, target).start()

    fetch[2].wait()
    spread_shape = (blocks, elements)
    spread = ones_where(lanes_of(spread_shape) // BLOCK_SIZE == rows_of(spread_shape))
    owner = jnp.broadcast_to((new_owner[...] - me).astype(F32), (8, blocks)).astype(BF16)
    away = dot(owner, spread)
    group = rows_of((8, elements))
    wanted = jnp.where(group <= SPREAD, group - SPREAD - 1, group - SPREAD)
    wanted = jnp.where(group == 0, 0, jnp.where(group > PEERS, 99, wanted)).astype(F32)
    match = jnp.where(away == wanted, 1.0, 0.0)
    square = (elements, elements)
    before = ones_where(rows_of(square) < lanes_of(square))
    place = dot(match.astype(BF16), before)
    counts = jnp.sum(match, axis=1, keepdims=True)
    keep_match = jnp.where(group == 0, match, 0.0)
    move_match = match - keep_match
    base = (MOVE * (group - 1)).astype(F32)
    kept = jnp.sum(keep_match * (place + 1.0), axis=0, keepdims=True).astype(jnp.int32) - 1
    moved = jnp.sum(move_match * (place + base + 1.0), axis=0, keepdims=True).astype(jnp.int32) - 1
    total = PEERS * MOVE
    move_sel = ones_where(rows_of((total, elements)) == moved)

    field_high, field_low = split(fields[...])
    outgoing = dot_nt(move_sel, field_high) + dot_nt(move_sel, field_low)
    for slot in range(PEERS):
        move_out[slot] = outgoing[MOVE * slot : MOVE * slot + MOVE, :]

    def moves(slot):
        return peer_copy(move_out.at[slot], move_in, move_send, move_recv, slot)

    start_all(moves)
    for n in (1, 3, 4, 6):
        fetch[n].wait()

    for slot in range(PEERS):

        @pl.when(jnp.logical_not(inside[slot]))
        def _():
            move_in[slot] = jnp.zeros(move_in.shape[1:], F32)
            force_in[slot] = jnp.zeros(force_in.shape[1:], F32)

    keep_sel = ones_where(rows_of(square) == kept)
    stays = dot_nt(field_high, keep_sel) + dot_nt(field_low, keep_sel)
    arrive = []
    start = counts[0:1, :]
    part_shape = (MOVE, elements)
    for slot in range(PEERS):
        number = rows_of(part_shape).astype(F32)
        count = counts[slot + 1 : slot + 2, :]
        hit = (lanes_of(part_shape).astype(F32) == start + number) & (number < count)
        arrive.append(jnp.where(hit, 1.0, 0.0))
        start = start + count
    arrive = jnp.concatenate(arrive, axis=0).astype(BF16)

    def arrived(ref):
        rows = jnp.concatenate([ref[slot] for slot in range(PEERS)], axis=0)
        high, low = split(rows.T)
        return dot(high, arrive) + dot(low, arrive)

    @pl.when(acoustic)
    def _():
        row_list[...] = jnp.full(row_list.shape, -1, jnp.int32)
        row_list[:, 0 : PEERS * FACE_CAP] = send_list[...]
        lane = rows_of((LANES, elements))
        entry = (PEERS - 1 - lane // FACE_CAP) * FACE_CAP + lane % FACE_CAP
        entry = jnp.where(lane < PEERS * FACE_CAP, entry + 6 * elements, -7)
        for face in range(6):
            slots = face_slot[face : face + 1, :]
            near[face] = ones_where(rows_of(square) + (face ^ 1) * elements == slots)
            far[:, elements * face : elements * face + elements] = ones_where(entry == slots)
            shape = (elements, LANES)
            sends[elements * face : elements * face + elements, :] = ones_where(
                rows_of(shape) + face * elements == row_list[...]
            )

    relayed = {this: [(t, c) for source, t, c in routes if source == this] for this in range(1, n_sec)}
    for this in range(1, n_sec):
        if relayed[this]:

            @pl.when(sec == this)
            def _():
                for target, chunk in relayed[this]:
                    lamb_copy(chunk, target).wait_recv()
                    lamb_copy(chunk, target).start()

    wait_recv_all(move_in, move_recv, move_send)
    out[...] = stays + arrived(move_in)

    @pl.when(acoustic)
    def _():
        lane = lanes_of((TRACE, LANES))
        for segment in range(SEGMENTS):

            def faces(slot):
                return peer_copy(
                    sent.at[segment], received.at[segment], face_send.at[segment], face_recv.at[segment], slot
                )

            if segment == 0:
                high, low = split(out[...])
                shown[...] = dot(pick[...], high) + dot(pick[...], low)
            shown_high, shown_low = split(shown[...])
            pairs = [
                jnp.concatenate(
                    [shown_high[TRACE * f : TRACE * f + TRACE], shown_low[TRACE * f : TRACE * f + TRACE]], axis=0
                )
                for f in range(6)
            ]
            listed = dot(jnp.concatenate(pairs, axis=1), sends[...])
            sent[segment] = listed[:TRACE] + listed[TRACE:]
            start_all(faces)
            if segment > 0:
                advance(segment - 1)
                high, low = split(out[...])
            beside = [dot(pairs[f ^ 1], near[f]) for f in range(6)]
            beside_pair = jnp.concatenate(beside, axis=0).astype(BF16)
            rate = dot(own_high[...], high) + dot(own_high[...], low) + dot(own_low[...], high)
            rate = rate + dot(lift[...], beside_pair)
            if segment == 0:
                source = ones_where(rows_of(square) == source_map[...])
                force_sel = dot_nt(move_sel, source).astype(BF16)
                stay_sel = dot_nt(source, keep_sel).astype(BF16)
                for this in range(1, n_sec):

                    @pl.when(sec == this)
                    def _():
                        early = [chunk for _, chunk in relayed[this]]
                        for chunk in range(CHUNKS):
                            if chunk not in early:
                                lamb_copy(chunk, 0).wait_recv()

                lamb_high, lamb_low = split(lamb[...])
                leaving = dot_nt(force_sel, lamb_high) + dot_nt(force_sel, lamb_low)
                for slot in range(PEERS):
                    force_out[slot] = leaving[MOVE * slot : MOVE * slot + MOVE, :]

                def forces(slot):
                    return peer_copy(force_out.at[slot], force_in, force_send, force_recv, slot)

                start_all(forces)
                stays_force = dot(lamb_high, stay_sel) + dot(lamb_low, stay_sel)
                wait_recv_all(force_in, force_recv, force_send)
                forced = stays_force + arrived(force_in)
                forced_high, forced_low = split(forced)
                force[SHOWN:, :] = forced
                force[:SHOWN, :] = dot(pick[:, 64:], forced_high) + dot(pick[:, 64:], forced_low)
            wait_recv_all(received.at[segment], face_recv.at[segment], face_send.at[segment])
            merged = jnp.zeros((TRACE, LANES), F32)
            for slot in range(PEERS):
                first = (PEERS - 1 - slot) * FACE_CAP
                here = (lane >= first) & (lane < first + FACE_CAP) & inside[slot]
                merged = jnp.where(here, received[segment, slot], merged)
            merged_high, merged_low = split(merged)
            remote = dot(jnp.concatenate([merged_high, merged_low], axis=0), far[...])
            remote = [remote[:, elements * f : elements * f + elements] for f in range(6)]
            remote_pair = jnp.concatenate(remote, axis=0).astype(BF16)
            if segment < SEGMENTS - 1:
                seen = rate[:SHOWN] + force[:SHOWN, :]
                seen = seen + dot(lift[:SHOWN, :], remote_pair)
                now = TIME_STEP * seen
                if segment > 0:
                    now = SEGMENT_CARRY[segment] * shown_carry[...] + now
                shown_carry[...] = now
                shown[...] = shown[...] + SEGMENT_WEIGHTS[segment] * now

            def advance(number, rate=rate, remote_pair=remote_pair):
                gain = rate[SHOWN:] + dot(lift[SHOWN:, :], remote_pair)
                gain = jnp.concatenate([gain[:64], gain[64:] + force[SHOWN:, :]], axis=0)
                step = TIME_STEP * gain
                if number > 0:
                    step = SEGMENT_CARRY[number] * carry[...] + step
                carry[...] = step
                out[...] = out[...] + SEGMENT_WEIGHTS[number] * step

        advance(SEGMENTS - 1)

        for segment in range(SEGMENTS):
            wait_send_all(
                lambda slot: peer_copy(
                    sent.at[segment], received.at[segment], face_send.at[segment], face_recv.at[segment], slot
                )
            )
        wait_send_all(lambda slot: peer_copy(force_out.at[slot], force_in, force_send, force_recv, slot))

    wait_send_all(moves)

    for this in range(n_sec):

        @pl.when(sec == this)
        def _():
            for source, target, chunk in routes:
                if source == this:
                    lamb_copy(chunk, target).wait_send()


def local(n_sec, n_dom, fields, source_map, new_owner, send_list, face_slot):
    rows = fields.shape[0] * fields.shape[1]
    elements = fields.shape[2]
    dma = pltpu.SemaphoreType.DMA
    vmem = pltpu.VMEM
    consts = [jnp.asarray(m) for m in constants()]
    operands = [
        fields.reshape(rows, elements),
        source_map.reshape(1, -1),
        new_owner.reshape(1, -1),
        send_list.reshape(1, -1),
        face_slot,
        *consts,
    ]
    call = pl.pallas_call(
        functools.partial(kernel, n_sec, n_dom),
        out_shape=jax.ShapeDtypeStruct((rows, elements), F32),
        in_specs=[pl.BlockSpec(memory_space=pltpu.HBM)] * INPUTS,
        out_specs=pl.BlockSpec(memory_space=pltpu.VMEM),
        scratch_shapes=[
            *[vmem(value.shape, value.dtype) for value in operands],
            vmem((rows, elements), F32),
            vmem((SHOWN + 192, elements), F32),
            vmem((SHOWN, elements), F32),
            vmem((SHOWN, elements), F32),
            vmem((192, elements), F32),
            vmem((6, elements, elements), BF16),
            vmem((LANES, 6 * elements), BF16),
            vmem((6 * elements, LANES), BF16),
            vmem((1, LANES), jnp.int32),
            vmem((PEERS, MOVE, rows), F32),
            vmem((PEERS, MOVE, rows), F32),
            vmem((PEERS, MOVE, 192), F32),
            vmem((PEERS, MOVE, 192), F32),
            vmem((SEGMENTS, TRACE, LANES), F32),
            vmem((SEGMENTS, PEERS, TRACE, LANES), F32),
            dma((INPUTS,)),
            dma((CHUNKS, n_sec)),
            dma((CHUNKS,)),
            dma((PEERS,)),
            dma((PEERS,)),
            dma((PEERS,)),
            dma((PEERS,)),
            dma((SEGMENTS, PEERS)),
            dma((SEGMENTS, PEERS)),
        ],
        compiler_params=pltpu.CompilerParams(
            collective_id=0, has_side_effects=True, vmem_limit_bytes=63 * 2**20
        ),
        name="step",
    )
    made = call(*operands)
    return made.reshape(fields.shape)


def solution(mesh):
    both = ("sec", "dom")
    in_specs = (P(None, None, both), P(both), P(both), P(both), P(None, both))
    run = functools.partial(local, mesh.shape["sec"], mesh.shape["dom"])
    return jax.shard_map(
        run, mesh=mesh, in_specs=in_specs, out_specs=P(None, None, both), check_vma=False
    )
```
